768 devices in a mesh: row: 384 (over z, y, x), col: 2 (over core).
Axes of the slice: x: 4, y: 8, z: 12, core: 2. Of those that a mesh axis runs over, the one named last changes fastest.
Arguments:
- three_center: bfloat16 [12288, 128, 512], P('row', None, 'col'), may hold values from -6 to 6
- screen_mask: int32 [12288, 2], P('row'), may hold values 0 or 1
- green_occ: bfloat16 [128, 128], replicated, may hold values from -0.5 to 0.5
- green_virt: bfloat16 [128, 128], replicated, may hold values from -0.5 to 0.5
Outputs:
- polariz: float32 [512, 512], P('col')
The draws below stay inside these ranges and needn't reach their ends.
All inputs are finite; a program needn't handle non-finite values. No bound on the sum of `screen_mask` on one device may be relied on, other than what follows from the above.
Results may differ from the reference program's by a relative error of at most 0.0041.
Values may be sent and summed in bfloat16 or wider, within the bound.
No kernel may reach another device: no remote copies, remote signals or barrier semaphores. Data moves between devices by JAX's collectives and lax.ppermute only.
A program may use at most 32 MiB of HBM per device.

```python
import jax
import jax.numpy as jnp
from jax import lax

NU = 128
NBLK = 64
NMU = 12288
NP = 512
N_ROW = 384


def with_ends(entries, key, smallest, largest):
    longest = entries.shape.index(max(entries.shape))
    spots = []
    for shift in (0, 1):
        where = [jax.random.randint(jax.random.fold_in(key, axis), (), 0, length) for axis, length in enumerate(entries.shape)]
        where[longest] = (where[longest] + shift) % entries.shape[longest]
        spots.append(tuple(where))
    return entries.at[spots[0]].set(smallest).at[spots[1]].set(largest)


def shard_levels(rng, shape, cuts, least, largest):
    def one(dim, shards_of):
        heights = jax.random.uniform(jax.random.fold_in(jax.random.fold_in(rng, 6), dim), (shards_of,), jnp.float32, least / len(cuts), largest / len(cuts))
        return jnp.repeat(jnp.exp(heights), shape[dim] // shards_of).reshape((-1,) + (1,) * (len(shape) - dim - 1))

    level = one(*cuts[0])
    for cut in cuts[1:]:
        level = level * one(*cut)
    return level


def centred(key, shape, scale, bound, split=(), held_as=jnp.bfloat16):
    level = shard_levels(key, shape, split, -0.22, 0.18) if split else 1.0
    drawn = jax.random.normal(key, shape, jnp.float32) * scale * level
    return jnp.minimum(jnp.maximum(drawn, -bound), bound).astype(held_as)


def setup_inputs(seed: int = 0) -> dict:
    key_list = jax.random.split(jax.random.key(seed), 5)
    return {
        "three_center": centred(key_list[0], (NMU, NU, NP), 1.0, 6.0, ((0, 384), (2, 2))),
        "screen_mask": with_ends((jax.random.randint(key_list[1], (NMU, NU // NBLK), 0, 4) < 3).astype(jnp.int32), jax.random.fold_in(key_list[1], 1), 0, 1),
        "green_occ": centred(key_list[2], (NU, NU), NU ** -0.5, 0.5),
        "green_virt": centred(key_list[3], (NU, NU), NU ** -0.5, 0.5),
    }


def reference(three_center, screen_mask, green_occ, green_virt):
    nmu, width, nrif = three_center.shape
    blocks = screen_mask.shape[1]
    keep = jnp.repeat(screen_mask, width // blocks, axis=1).astype(jnp.bfloat16)
    screened = three_center * keep[:, :, None]
    pieces = screened.reshape(N_ROW, nmu // N_ROW, width, nrif)
    occ_f = green_occ.astype(jnp.float32)
    virt_f = green_virt.astype(jnp.float32)
    high = lax.Precision.HIGHEST

    def step(total, piece):
        piece_f = piece.astype(jnp.float32)
        occ_side = jnp.einsum('sn,mnp->msp', occ_f, piece_f, precision=high).astype(jnp.bfloat16)
        virt_side = jnp.einsum('sn,mnp->msp', virt_f, piece_f, precision=high).astype(jnp.bfloat16)
        term = jnp.einsum('msp,msq->pq', occ_side.astype(jnp.float32), virt_side.astype(jnp.float32), precision=high)
        return (total + term, None)
    total, _ = lax.scan(step, jnp.zeros((nrif, nrif), jnp.float32), pieces)
    return -total / jnp.sqrt(jnp.float32(nmu * width))
```

```python
import jax
import jax.numpy as jnp
from jax import lax
from jax.sharding import Mesh, PartitionSpec as P

Z, YX = 12, 32


def contract(green, screened):
    return jnp.einsum("sn,mnp->msp", green, screened, preferred_element_type=jnp.float32).astype(
        jnp.bfloat16
    )


def pair(occ_side, virt_side):
    return jnp.einsum("msp,msq->pq", occ_side, virt_side, preferred_element_type=jnp.float32)


def sum_over_row(partial):
    rows, columns = partial.shape
    pieces = partial.astype(jnp.bfloat16).reshape(YX, rows // YX, columns)
    pieces = lax.all_to_all(pieces, "yx", 0, 0, tiled=True)
    piece = jnp.sum(pieces.astype(jnp.float32), axis=0).astype(jnp.bfloat16)
    copies = jnp.broadcast_to(piece[None], (Z,) + piece.shape)
    copies = lax.all_to_all(copies, "z", 0, 0, tiled=True)
    total = jnp.sum(copies.astype(jnp.float32), axis=0).astype(jnp.bfloat16)
    copies = jnp.broadcast_to(total[None], (YX,) + total.shape)
    return lax.all_to_all(copies, "yx", 0, 0, tiled=True).reshape(rows, columns)


def on_device(three_center, screen_mask, green_occ, green_virt):
    mu_dev, width, p_dev = three_center.shape
    blocks = screen_mask.shape[1]
    other = lax.ppermute(three_center, "col", [(0, 1), (1, 0)])
    keep = jnp.repeat(screen_mask, width // blocks, axis=1).astype(jnp.bfloat16)[:, :, None]
    mine = three_center * keep
    occ_side = contract(green_occ, mine)
    here = pair(occ_side, contract(green_virt, mine))
    there = pair(occ_side, contract(green_virt, other * keep))
    first = lax.axis_index("col") == 0
    partial = jnp.where(
        first, jnp.concatenate([here, there], axis=1), jnp.concatenate([there, here], axis=1)
    )
    summed = sum_over_row(partial).astype(jnp.float32)
    return -summed / jnp.sqrt(jnp.float32(mu_dev * Z * YX * width))


def solution(mesh):
    fine = Mesh(mesh.devices.reshape(Z, YX, 2), ("z", "yx", "col"))
    return jax.shard_map(
        on_device,
        mesh=fine,
        in_specs=(P(("z", "yx"), None, "col"), P(("z", "yx"), None), P(), P()),
        out_specs=P("col", None),
        check_vma=False,
    )
```

```python
import jax
import jax.numpy as jnp
from jax import lax
from jax.experimental import pallas as pl
from jax.experimental.pallas import tpu as pltpu
from jax.sharding import Mesh, PartitionSpec as P

Z, YX = 12, 32
CHUNKS = 4
VMEM = pl.BlockSpec(memory_space=pltpu.VMEM)
SMEM = pl.BlockSpec(memory_space=pltpu.SMEM)
HBM = pl.BlockSpec(memory_space=pltpu.HBM)
PARAMS = pltpu.CompilerParams(vmem_limit_bytes=32 * 2**20)


def masked(x, keep_ref, m):
    half = x.shape[0] // 2
    zero = jnp.zeros((half, x.shape[1]), x.dtype)
    return jnp.concatenate(
        [
            jnp.where(keep_ref[0, m] != 0, x[:half], zero),
            jnp.where(keep_ref[1, m] != 0, x[half:], zero),
        ],
        axis=0,
    )


def local_kernel(keep_hbm, occ_hbm, virt_hbm, x_hbm, occ_ref, here_ref, keep, green, x, virt, sems):
    count, width, _ = x.shape
    per_chunk = count // CHUNKS

    def chunk(c):
        part = pl.ds(c * per_chunk, per_chunk)
        return pltpu.make_async_copy(x_hbm.at[part], x.at[part], sems.at[c])

    small = [
        pltpu.make_async_copy(keep_hbm, keep, sems.at[CHUNKS]),
        pltpu.make_async_copy(occ_hbm, green.at[pl.ds(0, width)], sems.at[CHUNKS + 1]),
        pltpu.make_async_copy(virt_hbm, green.at[pl.ds(width, width)], sems.at[CHUNKS + 2]),
    ]
    for copy in small:
        copy.start()
    for c in range(CHUNKS):
        chunk(c).start()
    for copy in small:
        copy.wait()
    for c in range(CHUNKS):
        chunk(c).wait()
        for m in range(c * per_chunk, (c + 1) * per_chunk):
            both = jnp.dot(green[...], masked(x[m], keep, m), preferred_element_type=jnp.float32)
            both = both.astype(jnp.bfloat16)
            occ_ref[:, m * width : (m + 1) * width] = both[:width].T
            virt[m * width : (m + 1) * width, :] = both[width:]
    here = jnp.dot(occ_ref[...], virt[...], preferred_element_type=jnp.float32)
    here_ref[...] = here.astype(jnp.bfloat16)


def local_part(three_center, keep, green_occ, green_virt):
    count, width, own = three_center.shape
    args = (keep, green_occ, green_virt, three_center)
    return pl.pallas_call(
        local_kernel,
        in_specs=[HBM] * 4,
        out_specs=[VMEM, VMEM],
        out_shape=[
            jax.ShapeDtypeStruct((own, count * width), jnp.bfloat16),
            jax.ShapeDtypeStruct((own, own), jnp.bfloat16),
        ],
        scratch_shapes=[
            pltpu.SMEM(keep.shape, keep.dtype),
            pltpu.VMEM((2 * width, width), jnp.bfloat16),
            pltpu.VMEM(three_center.shape, jnp.bfloat16),
            pltpu.VMEM((count * width, own), jnp.bfloat16),
            pltpu.SemaphoreType.DMA((CHUNKS + 3,)),
        ],
        compiler_params=PARAMS,
    )(*[pltpu.with_memory_space_constraint(a, pltpu.HBM) for a in args])


def remote_kernel(keep, first_ref, green_ref, x_ref, occ_ref, here_ref, out_ref, virt):
    count, width, own = x_ref.shape
    green = green_ref[...]
    for m in range(count):
        side = jnp.dot(green, masked(x_ref[m], keep, m), preferred_element_type=jnp.float32)
        virt[m * width : (m + 1) * width, :] = side.astype(jnp.bfloat16)
    there = jnp.dot(occ_ref[...], virt[...], preferred_element_type=jnp.float32)
    there = there.astype(jnp.bfloat16)
    here = here_ref[...]
    first = first_ref[0] != 0
    out_ref[:, :own] = jnp.where(first, here, there)
    out_ref[:, own:] = jnp.where(first, there, here)


def remote_part(other, keep, first, green_virt, occ_side, here):
    count, width, own = other.shape
    return pl.pallas_call(
        remote_kernel,
        in_specs=[SMEM, SMEM, VMEM, VMEM, VMEM, VMEM],
        out_specs=VMEM,
        out_shape=jax.ShapeDtypeStruct((own, 2 * own), jnp.bfloat16),
        scratch_shapes=[pltpu.VMEM((count * width, own), jnp.bfloat16)],
        compiler_params=PARAMS,
    )(keep, first, green_virt, other, occ_side, here)


def sum_over_row(partial):
    rows, columns = partial.shape
    pieces = partial.reshape(YX, rows // YX, columns)
    pieces = lax.all_to_all(pieces, "yx", 0, 0, tiled=True)
    piece = jnp.sum(pieces.astype(jnp.float32), axis=0).astype(jnp.bfloat16)
    copies = jnp.broadcast_to(piece[None], (Z,) + piece.shape)
    copies = lax.all_to_all(copies, "z", 0, 0, tiled=True)
    total = jnp.sum(copies.astype(jnp.float32), axis=0).astype(jnp.bfloat16)
    copies = jnp.broadcast_to(total[None], (YX,) + total.shape)
    return lax.all_to_all(copies, "yx", 0, 0, tiled=True).reshape(rows, columns)


def on_device(three_center, screen_mask, green_occ, green_virt):
    mu_dev, width, _ = three_center.shape
    other = lax.ppermute(three_center, "col", [(0, 1), (1, 0)])
    keep = screen_mask.T
    occ_side, here = local_part(three_center, keep, green_occ, green_virt)
    first = (lax.axis_index("col") == 0).astype(jnp.int32).reshape(1)
    partial = remote_part(other, keep, first, green_virt, occ_side, here)
    summed = sum_over_row(partial).astype(jnp.float32)
    return -summed / jnp.sqrt(jnp.float32(mu_dev * Z * YX * width))


def solution(mesh):
    fine = Mesh(mesh.devices.reshape(Z, YX, 2), ("z", "yx", "col"))
    return jax.shard_map(
        on_device,
        mesh=fine,
        in_specs=(P(("z", "yx"), None, "col"), P(("z", "yx"), None), P(), P()),
        out_specs=P("col", None),
        check_vma=False,
    )
```

```python
import jax
import jax.numpy as jnp
from jax import lax
from jax.experimental import pallas as pl
from jax.experimental.pallas import tpu as pltpu
from jax.sharding import Mesh, PartitionSpec as P

Z, YX = 12, 32
CHUNKS = 4
VMEM = pl.BlockSpec(memory_space=pltpu.VMEM)
HBM = pl.BlockSpec(memory_space=pltpu.HBM)
PARAMS = pltpu.CompilerParams(vmem_limit_bytes=32 * 2**20)


def transposed_dot(a, b):
    return lax.dot_general(a, b, (((0,), (0,)), ((), ())), preferred_element_type=jnp.float32)


def local_kernel(
    keep_hbm, occ_hbm, virt_hbm, x_hbm, occ_ref, here_ref, kept_ref,
    keep, green, table, x, virt, sems,
):
    count, width, _ = x.shape
    per_chunk = count // CHUNKS

    def chunk(c):
        part = pl.ds(c * per_chunk, per_chunk)
        return pltpu.make_async_copy(x_hbm.at[part], x.at[part], sems.at[c])

    small = [
        pltpu.make_async_copy(keep_hbm, keep, sems.at[CHUNKS]),
        pltpu.make_async_copy(occ_hbm, green.at[pl.ds(0, width)], sems.at[CHUNKS + 1]),
        pltpu.make_async_copy(virt_hbm, green.at[pl.ds(width, width)], sems.at[CHUNKS + 2]),
    ]
    for copy in small:
        copy.start()
    for c in range(CHUNKS):
        chunk(c).start()
    for copy in small:
        copy.wait()
    whole = green[...]
    zero = jnp.zeros_like(whole)
    lower = lax.broadcasted_iota(jnp.int32, whole.shape, 1) < width // 2
    table[0] = zero
    table[1] = jnp.where(lower, zero, whole)
    table[2] = jnp.where(lower, whole, zero)
    table[3] = whole
    here = jnp.zeros(here_ref.shape, jnp.float32)
    for c in range(CHUNKS):
        chunk(c).wait()
        for m in range(c * per_chunk, (c + 1) * per_chunk):
            rows = pl.ds(m * width, width)
            which = jnp.where(keep[0, m] != 0, 2, 0) + jnp.where(keep[1, m] != 0, 1, 0)
            kept = table[which]
            kept_ref[m] = kept[width:]
            both = jnp.dot(kept, x[m], preferred_element_type=jnp.float32).astype(jnp.bfloat16)
            occ_ref[rows, :] = both[:width]
            virt[rows, :] = both[width:]
        rows = pl.ds(c * per_chunk * width, per_chunk * width)
        here = here + transposed_dot(occ_ref[rows, :], virt[rows, :])
    here_ref[...] = here.astype(jnp.bfloat16)


def local_part(three_center, keep, green_occ, green_virt):
    count, width, own = three_center.shape
    args = (keep, green_occ, green_virt, three_center)
    return pl.pallas_call(
        local_kernel,
        in_specs=[HBM] * 4,
        out_specs=[VMEM] * 3,
        out_shape=[
            jax.ShapeDtypeStruct((count * width, own), jnp.bfloat16),
            jax.ShapeDtypeStruct((own, own), jnp.bfloat16),
            jax.ShapeDtypeStruct((count, width, width), jnp.bfloat16),
        ],
        scratch_shapes=[
            pltpu.SMEM(keep.shape, keep.dtype),
            pltpu.VMEM((2 * width, width), jnp.bfloat16),
            pltpu.VMEM((4, 2 * width, width), jnp.bfloat16),
            pltpu.VMEM(three_center.shape, jnp.bfloat16),
            pltpu.VMEM((count * width, own), jnp.bfloat16),
            pltpu.SemaphoreType.DMA((CHUNKS + 3,)),
        ],
        compiler_params=PARAMS,
    )(*[pltpu.with_memory_space_constraint(a, pltpu.HBM) for a in args])


def remote_kernel(kept_ref, x_ref, occ_ref, here_ref, out_ref, virt):
    count, width, own = x_ref.shape
    for m in range(count):
        side = jnp.dot(kept_ref[m], x_ref[m], preferred_element_type=jnp.float32)
        virt[m * width : (m + 1) * width, :] = side.astype(jnp.bfloat16)
    out_ref[:, :own] = here_ref[...]
    out_ref[:, own:] = transposed_dot(occ_ref[...], virt[...]).astype(jnp.bfloat16)


def remote_part(other, kept, occ_side, here):
    count, width, own = other.shape
    return pl.pallas_call(
        remote_kernel,
        in_specs=[VMEM] * 4,
        out_specs=VMEM,
        out_shape=jax.ShapeDtypeStruct((own, 2 * own), jnp.bfloat16),
        scratch_shapes=[pltpu.VMEM((count * width, own), jnp.bfloat16)],
        compiler_params=PARAMS,
    )(kept, other, occ_side, here)


def sum_over_row(partial):
    rows, columns = partial.shape
    pieces = partial.reshape(YX, rows // YX, columns)
    pieces = lax.all_to_all(pieces, "yx", 0, 0, tiled=True)
    piece = jnp.sum(pieces.astype(jnp.float32), axis=0).astype(jnp.bfloat16)
    copies = jnp.broadcast_to(piece[None], (Z,) + piece.shape)
    copies = lax.all_to_all(copies, "z", 0, 0, tiled=True)
    total = jnp.sum(copies.astype(jnp.float32), axis=0).astype(jnp.bfloat16)
    copies = jnp.broadcast_to(total[None], (YX,) + total.shape)
    return lax.all_to_all(copies, "yx", 0, 0, tiled=True).reshape(rows, columns)


def on_device(three_center, screen_mask, green_occ, green_virt):
    mu_dev, width, own = three_center.shape
    other = lax.ppermute(three_center, "col", [(0, 1), (1, 0)])
    occ_side, here, kept = local_part(three_center, screen_mask.T, green_occ, green_virt)
    partial = remote_part(other, kept, occ_side, here)
    summed = sum_over_row(partial)
    swapped = jnp.concatenate([summed[:, own:], summed[:, :own]], axis=1)
    ordered = jnp.where(lax.axis_index("col") == 0, summed, swapped).astype(jnp.float32)
    return -ordered / jnp.sqrt(jnp.float32(mu_dev * Z * YX * width))


def solution(mesh):
    fine = Mesh(mesh.devices.reshape(Z, YX, 2), ("z", "yx", "col"))
    return jax.shard_map(
        on_device,
        mesh=fine,
        in_specs=(P(("z", "yx"), None, "col"), P(("z", "yx"), None), P(), P()),
        out_specs=P("col", None),
        check_vma=False,
    )
```

```python
import jax
import jax.numpy as jnp
from jax import lax
from jax.experimental import pallas as pl
from jax.experimental.pallas import tpu as pltpu
from jax.sharding import Mesh, PartitionSpec as P

Z, YX = 12, 32
CHUNKS = 4
VMEM = pl.BlockSpec(memory_space=pltpu.VMEM)
HBM = pl.BlockSpec(memory_space=pltpu.HBM)
PARAMS = pltpu.CompilerParams(vmem_limit_bytes=32 * 2**20)


def transposed_dot(a, b):
    return lax.dot_general(a, b, (((0,), (0,)), ((), ())), preferred_element_type=jnp.float32)


def local_kernel(
    keep_hbm, occ_hbm, virt_hbm, x_hbm, occ_ref, here_ref, kept_ref,
    keep, green, table, x, virt, sems,
):
    count, width, _ = x.shape
    per_chunk = count // CHUNKS

    def chunk(c):
        part = pl.ds(c * per_chunk, per_chunk)
        return pltpu.make_async_copy(x_hbm.at[part], x.at[part], sems.at[c])

    small = [
        pltpu.make_async_copy(keep_hbm, keep, sems.at[CHUNKS]),
        pltpu.make_async_copy(occ_hbm, green.at[pl.ds(0, width)], sems.at[CHUNKS + 1]),
        pltpu.make_async_copy(virt_hbm, green.at[pl.ds(width, width)], sems.at[CHUNKS + 2]),
    ]
    for copy in small:
        copy.start()
    for c in range(CHUNKS):
        chunk(c).start()
    for copy in small:
        copy.wait()
    whole = green[...]
    zero = jnp.zeros_like(whole)
    lower = lax.broadcasted_iota(jnp.int32, whole.shape, 1) < width // 2
    table[0] = zero
    table[1] = jnp.where(lower, zero, whole)
    table[2] = jnp.where(lower, whole, zero)
    table[3] = whole
    here = jnp.zeros(here_ref.shape, jnp.float32)
    for c in range(CHUNKS):
        chunk(c).wait()
        for m in range(c * per_chunk, (c + 1) * per_chunk):
            rows = pl.ds(m * width, width)
            which = jnp.where(keep[0, m] != 0, 2, 0) + jnp.where(keep[1, m] != 0, 1, 0)
            kept = table[which]
            kept_ref[m] = kept[width:]
            both = jnp.dot(kept, x[m], preferred_element_type=jnp.float32).astype(jnp.bfloat16)
            occ_ref[rows, :] = both[:width]
            virt[rows, :] = both[width:]
        rows = pl.ds(c * per_chunk * width, per_chunk * width)
        here = here + transposed_dot(occ_ref[rows, :], virt[rows, :])
    here_ref[...] = here.astype(jnp.bfloat16)


def local_part(three_center, keep, green_occ, green_virt):
    count, width, own = three_center.shape
    args = (keep, green_occ, green_virt, three_center)
    return pl.pallas_call(
        local_kernel,
        in_specs=[HBM] * 4,
        out_specs=[VMEM] * 3,
        out_shape=[
            jax.ShapeDtypeStruct((count * width, own), jnp.bfloat16),
            jax.ShapeDtypeStruct((own, own), jnp.bfloat16),
            jax.ShapeDtypeStruct((count, width, width), jnp.bfloat16),
        ],
        scratch_shapes=[
            pltpu.SMEM(keep.shape, keep.dtype),
            pltpu.VMEM((2 * width, width), jnp.bfloat16),
            pltpu.VMEM((4, 2 * width, width), jnp.bfloat16),
            pltpu.VMEM(three_center.shape, jnp.bfloat16),
            pltpu.VMEM((count * width, own), jnp.bfloat16),
            pltpu.SemaphoreType.DMA((CHUNKS + 3,)),
        ],
        compiler_params=PARAMS,
    )(*[pltpu.with_memory_space_constraint(a, pltpu.HBM) for a in args])


def remote_kernel(kept_ref, x_ref, occ_ref, here_ref, out_ref, virt):
    count, width, own = x_ref.shape
    for m in range(count):
        side = jnp.dot(kept_ref[m], x_ref[m], preferred_element_type=jnp.float32)
        virt[m * width : (m + 1) * width, :] = side.astype(jnp.bfloat16)
    there = transposed_dot(occ_ref[...], virt[...]).astype(jnp.bfloat16)
    here = here_ref[...]
    first = lax.axis_index("col") == 0
    out_ref[:, :own] = jnp.where(first, here, there)
    out_ref[:, own:] = jnp.where(first, there, here)


def remote_part(other, kept, occ_side, here):
    count, width, own = other.shape
    return pl.pallas_call(
        remote_kernel,
        in_specs=[VMEM] * 4,
        out_specs=VMEM,
        out_shape=jax.ShapeDtypeStruct((own, 2 * own), jnp.bfloat16),
        scratch_shapes=[pltpu.VMEM((count * width, own), jnp.bfloat16)],
        compiler_params=PARAMS,
    )(kept, other, occ_side, here)


def sum_over_row(partial):
    rows, columns = partial.shape
    pieces = partial.reshape(YX, rows // YX, columns)
    pieces = lax.all_to_all(pieces, "yx", 0, 0, tiled=True)
    piece = jnp.sum(pieces.astype(jnp.float32), axis=0).astype(jnp.bfloat16)
    copies = jnp.broadcast_to(piece[None], (Z,) + piece.shape)
    copies = lax.all_to_all(copies, "z", 0, 0, tiled=True)
    total = jnp.sum(copies.astype(jnp.float32), axis=0).astype(jnp.bfloat16)
    copies = jnp.broadcast_to(total[None], (YX,) + total.shape)
    return lax.all_to_all(copies, "yx", 0, 0, tiled=True).reshape(rows, columns)


def on_device(three_center, screen_mask, green_occ, green_virt):
    mu_dev, width, _ = three_center.shape
    other = lax.ppermute(three_center, "col", [(0, 1), (1, 0)])
    occ_side, here, kept = local_part(three_center, screen_mask.T, green_occ, green_virt)
    partial = remote_part(other, kept, occ_side, here)
    summed = sum_over_row(partial).astype(jnp.float32)
    return -summed / jnp.sqrt(jnp.float32(mu_dev * Z * YX * width))


def solution(mesh):
    fine = Mesh(mesh.devices.reshape(Z, YX, 2), ("z", "yx", "col"))
    return jax.shard_map(
        on_device,
        mesh=fine,
        in_specs=(P(("z", "yx"), None, "col"), P(("z", "yx"), None), P(), P()),
        out_specs=P("col", None),
        check_vma=False,
    )
```

```python
import jax
import jax.numpy as jnp
from jax import lax
from jax.experimental import pallas as pl
from jax.experimental.pallas import tpu as pltpu
from jax.sharding import Mesh, PartitionSpec as P

CUTS = {"z_hi": 3, "z_lo": 4, "y_hi": 4, "y_lo": 2, "x": 4}
NEAR, NEARS = ("y_lo", "x", "z_lo"), 32
FAR, FARS = ("y_hi", "z_hi"), 12
CHUNKS = 4
VMEM = pl.BlockSpec(memory_space=pltpu.VMEM)
HBM = pl.BlockSpec(memory_space=pltpu.HBM)
PARAMS = pltpu.CompilerParams(vmem_limit_bytes=32 * 2**20)


def transposed_dot(a, b):
    return lax.dot_general(a, b, (((0,), (0,)), ((), ())), preferred_element_type=jnp.float32)


def local_kernel(
    keep_hbm, occ_hbm, virt_hbm, x_hbm, occ_ref, here_ref, kept_ref,
    keep, green, table, x, virt, sems,
):
    count, width, _ = x.shape
    per_chunk = count // CHUNKS

    def chunk(c):
        part = pl.ds(c * per_chunk, per_chunk)
        return pltpu.make_async_copy(x_hbm.at[part], x.at[part], sems.at[c])

    small = [
        pltpu.make_async_copy(keep_hbm, keep, sems.at[CHUNKS]),
        pltpu.make_async_copy(occ_hbm, green.at[pl.ds(0, width)], sems.at[CHUNKS + 1]),
        pltpu.make_async_copy(virt_hbm, green.at[pl.ds(width, width)], sems.at[CHUNKS + 2]),
    ]
    for copy in small:
        copy.start()
    for c in range(CHUNKS):
        chunk(c).start()
    for copy in small:
        copy.wait()
    whole = green[...]
    zero = jnp.zeros_like(whole)
    lower = lax.broadcasted_iota(jnp.int32, whole.shape, 1) < width // 2
    table[0] = zero
    table[1] = jnp.where(lower, zero, whole)
    table[2] = jnp.where(lower, whole, zero)
    table[3] = whole
    here = jnp.zeros(here_ref.shape, jnp.float32)
    for c in range(CHUNKS):
        chunk(c).wait()
        for m in range(c * per_chunk, (c + 1) * per_chunk):
            rows = pl.ds(m * width, width)
            which = jnp.where(keep[0, m] != 0, 2, 0) + jnp.where(keep[1, m] != 0, 1, 0)
            kept = table[which]
            kept_ref[m] = kept[width:]
            both = jnp.dot(kept, x[m], preferred_element_type=jnp.float32).astype(jnp.bfloat16)
            occ_ref[rows, :] = both[:width]
            virt[rows, :] = both[width:]
        rows = pl.ds(c * per_chunk * width, per_chunk * width)
        here = here + transposed_dot(occ_ref[rows, :], virt[rows, :])
    here_ref[...] = here.astype(jnp.bfloat16)


def local_part(three_center, keep, green_occ, green_virt):
    count, width, own = three_center.shape
    args = (keep, green_occ, green_virt, three_center)
    return pl.pallas_call(
        local_kernel,
        in_specs=[HBM] * 4,
        out_specs=[VMEM] * 3,
        out_shape=[
            jax.ShapeDtypeStruct((count * width, own), jnp.bfloat16),
            jax.ShapeDtypeStruct((own, own), jnp.bfloat16),
            jax.ShapeDtypeStruct((count, width, width), jnp.bfloat16),
        ],
        scratch_shapes=[
            pltpu.SMEM(keep.shape, keep.dtype),
            pltpu.VMEM((2 * width, width), jnp.bfloat16),
            pltpu.VMEM((4, 2 * width, width), jnp.bfloat16),
            pltpu.VMEM(three_center.shape, jnp.bfloat16),
            pltpu.VMEM((count * width, own), jnp.bfloat16),
            pltpu.SemaphoreType.DMA((CHUNKS + 3,)),
        ],
        compiler_params=PARAMS,
    )(*[pltpu.with_memory_space_constraint(a, pltpu.HBM) for a in args])


def remote_kernel(kept_ref, x_ref, occ_ref, here_ref, out_ref, virt):
    count, width, own = x_ref.shape
    for m in range(count):
        side = jnp.dot(kept_ref[m], x_ref[m], preferred_element_type=jnp.float32)
        virt[m * width : (m + 1) * width, :] = side.astype(jnp.bfloat16)
    there = transposed_dot(occ_ref[...], virt[...]).astype(jnp.bfloat16)
    here = here_ref[...]
    first = lax.axis_index("col") == 0
    out_ref[:, :own] = jnp.where(first, here, there)
    out_ref[:, own:] = jnp.where(first, there, here)


def remote_part(other, kept, occ_side, here):
    count, width, own = other.shape
    return pl.pallas_call(
        remote_kernel,
        in_specs=[VMEM] * 4,
        out_specs=VMEM,
        out_shape=jax.ShapeDtypeStruct((own, 2 * own), jnp.bfloat16),
        scratch_shapes=[pltpu.VMEM((count * width, own), jnp.bfloat16)],
        compiler_params=PARAMS,
    )(kept, other, occ_side, here)


def sum_over_row(partial):
    rows, columns = partial.shape
    pieces = partial.reshape(NEARS, rows // NEARS, columns)
    pieces = lax.all_to_all(pieces, NEAR, 0, 0, tiled=True)
    piece = jnp.sum(pieces.astype(jnp.float32), axis=0).astype(jnp.bfloat16)
    copies = jnp.broadcast_to(piece[None], (FARS,) + piece.shape)
    copies = lax.all_to_all(copies, FAR, 0, 0, tiled=True)
    total = jnp.sum(copies.astype(jnp.float32), axis=0).astype(jnp.bfloat16)
    copies = jnp.broadcast_to(total[None], (NEARS,) + total.shape)
    return lax.all_to_all(copies, NEAR, 0, 0, tiled=True).reshape(rows, columns)


def on_device(three_center, screen_mask, green_occ, green_virt):
    mu_dev, width, _ = three_center.shape
    other = lax.ppermute(three_center, "col", [(0, 1), (1, 0)])
    occ_side, here, kept = local_part(three_center, screen_mask.T, green_occ, green_virt)
    partial = remote_part(other, kept, occ_side, here)
    summed = sum_over_row(partial).astype(jnp.float32)
    return -summed / jnp.sqrt(jnp.float32(mu_dev * NEARS * FARS * width))


def solution(mesh):
    row = tuple(CUTS)
    fine = Mesh(mesh.devices.reshape(*CUTS.values(), 2), row + ("col",))
    return jax.shard_map(
        on_device,
        mesh=fine,
        in_specs=(P(row, None, "col"), P(row, None), P(), P()),
        out_specs=P("col", None),
        check_vma=False,
    )
```

```python
import jax
import jax.numpy as jnp
from jax import lax
from jax.experimental import pallas as pl
from jax.experimental.pallas import tpu as pltpu
from jax.sharding import Mesh, PartitionSpec as P

Z, YX = 12, 32
CHUNKS = 4
VMEM = pl.BlockSpec(memory_space=pltpu.VMEM)
HBM = pl.BlockSpec(memory_space=pltpu.HBM)
PARAMS = pltpu.CompilerParams(vmem_limit_bytes=32 * 2**20)


def transposed_dot(a, b):
    return lax.dot_general(a, b, (((0,), (0,)), ((), ())), preferred_element_type=jnp.float32)


def local_kernel(
    keep_hbm, occ_hbm, virt_hbm, x_hbm, occ_ref, here_ref, kept_ref,
    keep, green, table, x, virt, sems,
):
    count, width, _ = x.shape
    per_chunk = count // CHUNKS

    def chunk(c):
        part = pl.ds(c * per_chunk, per_chunk)
        return pltpu.make_async_copy(x_hbm.at[part], x.at[part], sems.at[c])

    small = [
        pltpu.make_async_copy(keep_hbm, keep, sems.at[CHUNKS]),
        pltpu.make_async_copy(occ_hbm, green.at[pl.ds(0, width)], sems.at[CHUNKS + 1]),
        pltpu.make_async_copy(virt_hbm, green.at[pl.ds(width, width)], sems.at[CHUNKS + 2]),
    ]
    for copy in small:
        copy.start()
    for c in range(CHUNKS):
        chunk(c).start()
    for copy in small:
        copy.wait()
    whole = green[...]
    zero = jnp.zeros_like(whole)
    lower = lax.broadcasted_iota(jnp.int32, whole.shape, 1) < width // 2
    table[0] = zero
    table[1] = jnp.where(lower, zero, whole)
    table[2] = jnp.where(lower, whole, zero)
    table[3] = whole
    here = jnp.zeros(here_ref.shape, jnp.float32)
    for c in range(CHUNKS):
        chunk(c).wait()
        for m in range(c * per_chunk, (c + 1) * per_chunk):
            rows = pl.ds(m * width, width)
            which = jnp.where(keep[0, m] != 0, 2, 0) + jnp.where(keep[1, m] != 0, 1, 0)
            kept = table[which]
            kept_ref[m] = kept[width:]
            both = jnp.dot(kept, x[m], preferred_element_type=jnp.float32).astype(jnp.bfloat16)
            occ_ref[rows, :] = both[:width]
            virt[rows, :] = both[width:]
        rows = pl.ds(c * per_chunk * width, per_chunk * width)
        here = here + transposed_dot(occ_ref[rows, :], virt[rows, :])
    here_ref[...] = here.astype(jnp.bfloat16)


def local_part(three_center, keep, green_occ, green_virt):
    count, width, own = three_center.shape
    args = (keep, green_occ, green_virt, three_center)
    return pl.pallas_call(
        local_kernel,
        in_specs=[HBM] * 4,
        out_specs=[VMEM] * 3,
        out_shape=[
            jax.ShapeDtypeStruct((count * width, own), jnp.bfloat16),
            jax.ShapeDtypeStruct((own, own), jnp.bfloat16),
            jax.ShapeDtypeStruct((count, width, width), jnp.bfloat16),
        ],
        scratch_shapes=[
            pltpu.SMEM(keep.shape, keep.dtype),
            pltpu.VMEM((2 * width, width), jnp.bfloat16),
            pltpu.VMEM((4, 2 * width, width), jnp.bfloat16),
            pltpu.VMEM(three_center.shape, jnp.bfloat16),
            pltpu.VMEM((count * width, own), jnp.bfloat16),
            pltpu.SemaphoreType.DMA((CHUNKS + 3,)),
        ],
        compiler_params=PARAMS,
    )(*[pltpu.with_memory_space_constraint(a, pltpu.HBM) for a in args])


def remote_kernel(kept_ref, x_ref, occ_ref, out_ref, virt):
    count, width, _ = x_ref.shape
    for m in range(count):
        side = jnp.dot(kept_ref[m], x_ref[m], preferred_element_type=jnp.float32)
        virt[m * width : (m + 1) * width, :] = side.astype(jnp.bfloat16)
    out_ref[...] = transposed_dot(occ_ref[...], virt[...]).astype(jnp.bfloat16)


def remote_part(other, kept, occ_side):
    count, width, own = other.shape
    return pl.pallas_call(
        remote_kernel,
        in_specs=[VMEM] * 3,
        out_specs=VMEM,
        out_shape=jax.ShapeDtypeStruct((own, own), jnp.bfloat16),
        scratch_shapes=[pltpu.VMEM((count * width, own), jnp.bfloat16)],
        compiler_params=PARAMS,
    )(kept, other, occ_side)


def sum_over_row(partial):
    rows, columns = partial.shape
    pieces = partial.reshape(YX, rows // YX, columns)
    pieces = lax.all_to_all(pieces, "yx", 0, 0, tiled=True)
    piece = jnp.sum(pieces.astype(jnp.float32), axis=0).astype(jnp.bfloat16)
    copies = jnp.broadcast_to(piece[None], (Z,) + piece.shape)
    copies = lax.all_to_all(copies, "z", 0, 0, tiled=True)
    total = jnp.sum(copies.astype(jnp.float32), axis=0).astype(jnp.bfloat16)
    copies = jnp.broadcast_to(total[None], (YX,) + total.shape)
    return lax.all_to_all(copies, "yx", 0, 0, tiled=True).reshape(rows, columns)


def on_device(three_center, screen_mask, green_occ, green_virt):
    mu_dev, width, _ = three_center.shape
    other = lax.ppermute(three_center, "col", [(0, 1), (1, 0)])
    occ_side, here, kept = local_part(three_center, screen_mask.T, green_occ, green_virt)
    there = remote_part(other, kept, occ_side)
    here, there = sum_over_row(here), sum_over_row(there)
    first = lax.axis_index("col") == 0
    summed = jnp.concatenate(
        [jnp.where(first, here, there), jnp.where(first, there, here)], axis=1
    ).astype(jnp.float32)
    return -summed / jnp.sqrt(jnp.float32(mu_dev * Z * YX * width))


def solution(mesh):
    fine = Mesh(mesh.devices.reshape(Z, YX, 2), ("z", "yx", "col"))
    return jax.shard_map(
        on_device,
        mesh=fine,
        in_specs=(P(("z", "yx"), None, "col"), P(("z", "yx"), None), P(), P()),
        out_specs=P("col", None),
        check_vma=False,
    )
```

```python
import jax
import jax.numpy as jnp
from jax import lax
from jax.experimental import pallas as pl
from jax.experimental.pallas import tpu as pltpu
from jax.sharding import Mesh, PartitionSpec as P

Z, YX = 12, 32
CHUNKS = 4
VMEM = pl.BlockSpec(memory_space=pltpu.VMEM)
HBM = pl.BlockSpec(memory_space=pltpu.HBM)
PARAMS = pltpu.CompilerParams(vmem_limit_bytes=32 * 2**20)


def transposed_dot(a, b):
    return lax.dot_general(a, b, (((0,), (0,)), ((), ())), preferred_element_type=jnp.float32)


def local_kernel(
    keep_hbm, occ_hbm, virt_hbm, x_hbm, occ_ref, here_ref, kept_ref,
    keep, green, table, x, virt, sems,
):
    count, width, _ = x.shape
    per_chunk = count // CHUNKS

    def chunk(c):
        part = pl.ds(c * per_chunk, per_chunk)
        return pltpu.make_async_copy(x_hbm.at[part], x.at[part], sems.at[c])

    small = [
        pltpu.make_async_copy(keep_hbm, keep, sems.at[CHUNKS]),
        pltpu.make_async_copy(occ_hbm, green.at[pl.ds(0, width)], sems.at[CHUNKS + 1]),
        pltpu.make_async_copy(virt_hbm, green.at[pl.ds(width, width)], sems.at[CHUNKS + 2]),
    ]
    for copy in small:
        copy.start()
    for c in range(CHUNKS):
        chunk(c).start()
    for copy in small:
        copy.wait()
    whole = green[...]
    zero = jnp.zeros_like(whole)
    lower = lax.broadcasted_iota(jnp.int32, whole.shape, 1) < width // 2
    table[0] = zero
    table[1] = jnp.where(lower, zero, whole)
    table[2] = jnp.where(lower, whole, zero)
    table[3] = whole
    here = jnp.zeros(here_ref.shape, jnp.float32)
    for c in range(CHUNKS):
        chunk(c).wait()
        for m in range(c * per_chunk, (c + 1) * per_chunk):
            rows = pl.ds(m * width, width)
            which = jnp.where(keep[0, m] != 0, 2, 0) + jnp.where(keep[1, m] != 0, 1, 0)
            kept = table[which]
            kept_ref[m] = kept[width:]
            both = jnp.dot(kept, x[m], preferred_element_type=jnp.float32).astype(jnp.bfloat16)
            occ_ref[rows, :] = both[:width]
            virt[rows, :] = both[width:]
        rows = pl.ds(c * per_chunk * width, per_chunk * width)
        here = here + transposed_dot(occ_ref[rows, :], virt[rows, :])
    here_ref[...] = here.astype(jnp.bfloat16)


def local_part(three_center, keep, green_occ, green_virt):
    count, width, own = three_center.shape
    args = (keep, green_occ, green_virt, three_center)
    return pl.pallas_call(
        local_kernel,
        in_specs=[HBM] * 4,
        out_specs=[VMEM] * 3,
        out_shape=[
            jax.ShapeDtypeStruct((count * width, own), jnp.bfloat16),
            jax.ShapeDtypeStruct((own, own), jnp.bfloat16),
            jax.ShapeDtypeStruct((count, width, width), jnp.bfloat16),
        ],
        scratch_shapes=[
            pltpu.SMEM(keep.shape, keep.dtype),
            pltpu.VMEM((2 * width, width), jnp.bfloat16),
            pltpu.VMEM((4, 2 * width, width), jnp.bfloat16),
            pltpu.VMEM(three_center.shape, jnp.bfloat16),
            pltpu.VMEM((count * width, own), jnp.bfloat16),
            pltpu.SemaphoreType.DMA((CHUNKS + 3,)),
        ],
        compiler_params=PARAMS,
    )(*[pltpu.with_memory_space_constraint(a, pltpu.HBM) for a in args])


def remote_kernel(kept_ref, x_ref, occ_ref, here_ref, out_ref, virt):
    count, width, own = x_ref.shape
    for m in range(count):
        side = jnp.dot(kept_ref[m], x_ref[m], preferred_element_type=jnp.float32)
        virt[m * width : (m + 1) * width, :] = side.astype(jnp.bfloat16)
    there = transposed_dot(occ_ref[...], virt[...]).astype(jnp.bfloat16)
    here = here_ref[...]
    first = lax.axis_index("col") == 0
    out_ref[:, :own] = jnp.where(first, here, there)
    out_ref[:, own:] = jnp.where(first, there, here)


def remote_part(other, kept, occ_side, here):
    count, width, own = other.shape
    return pl.pallas_call(
        remote_kernel,
        in_specs=[VMEM] * 4,
        out_specs=VMEM,
        out_shape=jax.ShapeDtypeStruct((own, 2 * own), jnp.bfloat16),
        scratch_shapes=[pltpu.VMEM((count * width, own), jnp.bfloat16)],
        compiler_params=PARAMS,
    )(kept, other, occ_side, here)


def sum_over_row(partial):
    rows, columns = partial.shape
    pieces = partial.reshape(YX, rows // YX, columns)
    pieces = lax.all_to_all(pieces, "yx", 0, 0, tiled=True)
    piece = jnp.sum(pieces.astype(jnp.float32), axis=0).astype(jnp.bfloat16)
    copies = jnp.broadcast_to(piece[None], (Z,) + piece.shape)
    copies = lax.all_to_all(copies, ("z_lo", "z_hi"), 0, 0, tiled=True)
    total = jnp.sum(copies.astype(jnp.float32), axis=0).astype(jnp.bfloat16)
    copies = jnp.broadcast_to(total[None], (YX,) + total.shape)
    return lax.all_to_all(copies, "yx", 0, 0, tiled=True).reshape(rows, columns)


def on_device(three_center, screen_mask, green_occ, green_virt):
    mu_dev, width, _ = three_center.shape
    other = lax.ppermute(three_center, "col", [(0, 1), (1, 0)])
    occ_side, here, kept = local_part(three_center, screen_mask.T, green_occ, green_virt)
    partial = remote_part(other, kept, occ_side, here)
    summed = sum_over_row(partial).astype(jnp.float32)
    return -summed / jnp.sqrt(jnp.float32(mu_dev * Z * YX * width))


def solution(mesh):
    row = ("z_hi", "z_lo", "yx")
    fine = Mesh(mesh.devices.reshape(Z // 2, 2, YX, 2), ("z_hi", "z_lo", "yx", "col"))
    return jax.shard_map(
        on_device,
        mesh=fine,
        in_specs=(P(row, None, "col"), P(row, None), P(), P()),
        out_specs=P("col", None),
        check_vma=False,
    )
```

```python
import jax
import jax.numpy as jnp
from jax import lax
from jax.experimental import pallas as pl
from jax.experimental.pallas import tpu as pltpu
from jax.sharding import Mesh, PartitionSpec as P

Z, YX = 12, 32
CHUNKS = 4
VMEM = pl.BlockSpec(memory_space=pltpu.VMEM)
HBM = pl.BlockSpec(memory_space=pltpu.HBM)
PARAMS = pltpu.CompilerParams(vmem_limit_bytes=32 * 2**20)


def transposed_dot(a, b):
    return lax.dot_general(a, b, (((0,), (0,)), ((), ())), preferred_element_type=jnp.float32)


def local_kernel(
    keep_hbm, occ_hbm, virt_hbm, x_hbm, occ_ref, here_ref, kept_ref,
    keep, green, table, x, virt, sems,
):
    count, width, _ = x.shape
    per_chunk = count // CHUNKS

    def chunk(c):
        part = pl.ds(c * per_chunk, per_chunk)
        return pltpu.make_async_copy(x_hbm.at[part], x.at[part], sems.at[c])

    small = [
        pltpu.make_async_copy(keep_hbm, keep, sems.at[CHUNKS]),
        pltpu.make_async_copy(occ_hbm, green.at[pl.ds(0, width)], sems.at[CHUNKS + 1]),
        pltpu.make_async_copy(virt_hbm, green.at[pl.ds(width, width)], sems.at[CHUNKS + 2]),
    ]
    for copy in small:
        copy.start()
    for c in range(CHUNKS):
        chunk(c).start()
    for copy in small:
        copy.wait()
    whole = green[...]
    zero = jnp.zeros_like(whole)
    lower = lax.broadcasted_iota(jnp.int32, whole.shape, 1) < width // 2
    table[0] = zero
    table[1] = jnp.where(lower, zero, whole)
    table[2] = jnp.where(lower, whole, zero)
    table[3] = whole
    here = jnp.zeros(here_ref.shape, jnp.float32)
    for c in range(CHUNKS):
        chunk(c).wait()
        for m in range(c * per_chunk, (c + 1) * per_chunk):
            rows = pl.ds(m * width, width)
            which = jnp.where(keep[0, m] != 0, 2, 0) + jnp.where(keep[1, m] != 0, 1, 0)
            kept = table[which]
            kept_ref[m] = kept[width:]
            both = jnp.dot(kept, x[m], preferred_element_type=jnp.float32).astype(jnp.bfloat16)
            occ_ref[rows, :] = both[:width]
            virt[rows, :] = both[width:]
        rows = pl.ds(c * per_chunk * width, per_chunk * width)
        here = here + transposed_dot(occ_ref[rows, :], virt[rows, :])
    here_ref[...] = here.astype(jnp.bfloat16)


def local_part(three_center, keep, green_occ, green_virt):
    count, width, own = three_center.shape
    args = (keep, green_occ, green_virt, three_center)
    return pl.pallas_call(
        local_kernel,
        in_specs=[HBM] * 4,
        out_specs=[VMEM] * 3,
        out_shape=[
            jax.ShapeDtypeStruct((count * width, own), jnp.bfloat16),
            jax.ShapeDtypeStruct((own, own), jnp.bfloat16),
            jax.ShapeDtypeStruct((count, width, width), jnp.bfloat16),
        ],
        scratch_shapes=[
            pltpu.SMEM(keep.shape, keep.dtype),
            pltpu.VMEM((2 * width, width), jnp.bfloat16),
            pltpu.VMEM((4, 2 * width, width), jnp.bfloat16),
            pltpu.VMEM(three_center.shape, jnp.bfloat16),
            pltpu.VMEM((count * width, own), jnp.bfloat16),
            pltpu.SemaphoreType.DMA((CHUNKS + 3,)),
        ],
        compiler_params=PARAMS,
    )(*[pltpu.with_memory_space_constraint(a, pltpu.HBM) for a in args])


def remote_kernel(kept_ref, x_ref, occ_ref, here_ref, out_ref, virt):
    count, width, own = x_ref.shape
    for m in range(count):
        side = jnp.dot(kept_ref[m], x_ref[m], preferred_element_type=jnp.float32)
        virt[m * width : (m + 1) * width, :] = side.astype(jnp.bfloat16)
    there = transposed_dot(occ_ref[...], virt[...]).astype(jnp.bfloat16)
    here = here_ref[...]
    first = lax.axis_index("col") == 0
    out_ref[:, :own] = jnp.where(first, here, there)
    out_ref[:, own:] = jnp.where(first, there, here)


def remote_part(other, kept, occ_side, here):
    count, width, own = other.shape
    return pl.pallas_call(
        remote_kernel,
        in_specs=[VMEM] * 4,
        out_specs=VMEM,
        out_shape=jax.ShapeDtypeStruct((own, 2 * own), jnp.bfloat16),
        scratch_shapes=[pltpu.VMEM((count * width, own), jnp.bfloat16)],
        compiler_params=PARAMS,
    )(kept, other, occ_side, here)


def sum_over_row(partial):
    rows, columns = partial.shape
    pieces = partial.reshape(YX, rows // YX, columns)
    pieces = lax.all_to_all(pieces, "yx", 0, 0, tiled=True)
    piece = jnp.sum(pieces.astype(jnp.float32), axis=0).astype(jnp.bfloat16)
    copies = jnp.broadcast_to(piece[None], (Z,) + piece.shape)
    copies = lax.all_to_all(copies, ("z_lo", "z_hi"), 0, 0, tiled=True)
    total = jnp.sum(copies.astype(jnp.float32), axis=0).astype(jnp.bfloat16)
    copies = jnp.broadcast_to(total[None], (YX,) + total.shape)
    return lax.all_to_all(copies, "yx", 0, 0, tiled=True).reshape(rows, columns)


def on_device(three_center, screen_mask, green_occ, green_virt):
    mu_dev, width, _ = three_center.shape
    other = lax.ppermute(three_center, "col", [(0, 1), (1, 0)])
    occ_side, here, kept = local_part(three_center, screen_mask.T, green_occ, green_virt)
    partial = remote_part(other, kept, occ_side, here)
    summed = sum_over_row(partial).astype(jnp.float32)
    return -summed / jnp.sqrt(jnp.float32(mu_dev * Z * YX * width))


def solution(mesh):
    row = ("z_hi", "z_lo", "yx")
    fine = Mesh(mesh.devices.reshape(Z // 3, 3, YX, 2), ("z_hi", "z_lo", "yx", "col"))
    return jax.shard_map(
        on_device,
        mesh=fine,
        in_specs=(P(row, None, "col"), P(row, None), P(), P()),
        out_specs=P("col", None),
        check_vma=False,
    )
```
